768 devices in a mesh: section: 48 (over y, z_hi, core), mp: 16 (over z_lo, x).
Axes of the slice: x: 4, y: 8, z: 12 (z_hi: 3, z_lo: 4; z = z_hi * 4 + z_lo), core: 2. Of those that a mesh axis runs over, the one named last changes fastest.
Arguments:
- queries: bfloat16 [48, 256, 4096], P('section', None, 'mp'), may hold values from -80 to 80
- encoded: bfloat16 [48, 256, 4096], P('section', None, 'mp'), may hold values from -5 to 5
- key_weight: bfloat16 [48, 4096, 4096], P('section', None, 'mp'), may hold values from -1 to 2
- value_weight: bfloat16 [48, 4096, 4096], P('section', None, 'mp'), may hold values from -0.09375 to 0.09375
- owner: int32 [8], replicated, may hold values from 0 to 47, as said below
Outputs:
- passed: bfloat16 [48, 256, 4096], P('section', None, 'mp')
The draws below stay inside these ranges and needn't reach their ends.
Inputs may be any that keep to these rules, and one draw needn't show every extreme that they name: The 8 entries are distinct sections; owner[m] is the section whose block of encoded serves micro-batch m. Section 47 is always among them, and micro-batch 0 is always served by section 0.
All inputs are finite; a program needn't handle non-finite values.
Results may differ from the reference program's by a relative error of at most 0.011.
Values may be sent and summed in bfloat16 or wider, within the bound.
A program may use at most 32 MiB of HBM per device.

```python
import jax
import jax.numpy as jnp
from jax import lax

D = 4096
HEADS = 16
HEAD_DIM = 256
MICRO = 8
DEC_TOKENS = 256
ENC_TOKENS = 256
LOOP = 48


def owner_table(key):
    first_key = jax.random.fold_in(key, 11)
    second_key = jax.random.fold_in(key, 12)
    inner = jax.random.permutation(first_key, LOOP - 2)[:MICRO - 2] + 1
    others = jnp.concatenate([jnp.array([LOOP - 1], dtype=jnp.int32), inner.astype(jnp.int32)])
    order = jax.random.permutation(second_key, MICRO - 1)
    others = others[order]
    anchor = LOOP // 2 % MICRO
    table = jnp.concatenate([others[:anchor], jnp.array([0], dtype=jnp.int32), others[anchor:]])
    return table.astype(jnp.int32)


def encoded_table(key):
    base = jax.random.normal(jax.random.fold_in(key, 21), (LOOP, ENC_TOKENS, D), jnp.float32)
    base = jnp.clip(base, -5.0, 5.0)
    return base


def draw_owner(key, part):
    return owner_table(key)


def draw_encoded(key, part):
    return encoded_table(key).astype(jnp.bfloat16)


def draw_queries(key, part):
    base = jax.random.normal(jax.random.fold_in(key, 31), (LOOP, DEC_TOKENS, HEADS * HEAD_DIM), jnp.float32)
    base = jnp.clip(base, -5.0, 5.0)
    return base.astype(jnp.bfloat16)


def draw_key_weight(key, part):
    base = jax.random.normal(jax.random.fold_in(key, 41), (LOOP, D, HEADS * HEAD_DIM), jnp.float32)
    base = jnp.clip(base, -6.0, 6.0) * D ** (-0.5)
    return base.astype(jnp.bfloat16)


def levels(key, shape, shards, smallest, top_value):
    def one(position, parts):
        steps = jax.random.uniform(jax.random.fold_in(jax.random.fold_in(key, 6), position), (parts,), jnp.float32, smallest / len(shards), top_value / len(shards))
        return jnp.repeat(jnp.exp(steps), shape[position] // parts).reshape((-1,) + (1,) * (len(shape) - position - 1))

    gain = one(*shards[0])
    for cut in shards[1:]:
        gain = gain * one(*cut)
    return gain


def normal_values(own_key, shape, width, limit, cuts=(), held_as=jnp.bfloat16):
    drawn = jax.random.normal(own_key, shape, jnp.float32) * width
    if len(cuts) > 0:
        drawn = levels(own_key, shape, cuts, -0.22, 0.18) * drawn
    return jnp.clip(drawn, min=-limit, max=limit).astype(held_as)


def setup_inputs(seed: int = 0) -> dict:
    splits = jax.random.split(jax.random.key(seed), 6)
    queries = draw_queries(jax.random.fold_in(splits[5], 71), 0)
    encoded = draw_encoded(jax.random.fold_in(splits[5], 71), 0)
    key_weight = draw_key_weight(jax.random.fold_in(splits[5], 71), 0)
    value_weight = normal_values(splits[3], (LOOP, D, HEADS * HEAD_DIM), D ** -0.5, 0.09375, ((0, 48), (2, 16)))
    owner = draw_owner(jax.random.fold_in(splits[5], 71), 0)
    return dict(queries=queries, encoded=encoded, key_weight=key_weight, value_weight=value_weight, owner=owner)


def reference(queries, encoded, key_weight, value_weight, owner):
    scale = HEAD_DIM ** -0.5

    def one_section(section_id):
        micro_id = section_id % MICRO
        holder = owner[micro_id].astype(jnp.int32)
        block = lax.dynamic_index_in_dim(encoded, holder, 0, keepdims=False)
        w_key = lax.dynamic_index_in_dim(key_weight, section_id, 0, keepdims=False)
        w_value = lax.dynamic_index_in_dim(value_weight, section_id, 0, keepdims=False)
        keys = jnp.dot(block, w_key, preferred_element_type=jnp.float32).astype(jnp.bfloat16)
        values = jnp.dot(block, w_value, preferred_element_type=jnp.float32).astype(jnp.bfloat16)
        query = lax.dynamic_index_in_dim(queries, section_id, 0, keepdims=False)
        q_heads = query.astype(jnp.float32).reshape(DEC_TOKENS, HEADS, HEAD_DIM)
        k_heads = keys.astype(jnp.float32).reshape(ENC_TOKENS, HEADS, HEAD_DIM)
        v_heads = values.astype(jnp.float32).reshape(ENC_TOKENS, HEADS, HEAD_DIM)
        scores = jnp.einsum("thd,shd->hts", q_heads, k_heads) * scale
        probs = jax.nn.softmax(scores, axis=-1).astype(jnp.bfloat16)
        context = jnp.einsum("hts,shd->thd", probs.astype(jnp.float32), v_heads)
        return context.reshape(DEC_TOKENS, HEADS * HEAD_DIM).astype(jnp.bfloat16)

    contexts = lax.map(one_section, jnp.arange(LOOP, dtype=jnp.int32))
    return jnp.roll(contexts, 1, axis=0)
```

```python
import jax
import jax.numpy as jnp
from jax import lax
from jax.experimental import pallas as pl
from jax.experimental.pallas import tpu as pltpu
from jax.sharding import PartitionSpec as P

MESH = pl.DeviceIdType.MESH
HEAD_DIM = 256
MICRO = 8
NY, NZH, NC = 8, 3, 2
NZL, NX = 4, 4
PLANE = NY * NC
ROWS = 256
PIECE = ROWS // PLANE
HALF = 128
CHUNKS = 4
F32 = jnp.float32
BF16 = jnp.bfloat16


def kernel(q_hbm, e_hbm, wk_hbm, wv_hbm, owner_hbm, out_hbm,
           owner, q, wk, wv, p0, p1, c0, c1, f, e, acck, accv, ctx,
           own_sem, q_sem, w_sem, s1_send, s1_recv, s2_send, s2_recv, s3_send, s3_recv,
           z_send, x_send, g_recv, o_send, o_recv):
    sec = lax.axis_index("section")
    mp = lax.axis_index("mp")
    y, zh, c = lax.div(sec, 6), lax.rem(lax.div(sec, 2), 3), lax.rem(sec, 2)
    zl, x = lax.div(mp, 4), lax.rem(mp, 4)
    place = y * 2 + c
    right = zl * 4 + lax.rem(x + 1, 4)
    left = zl * 4 + lax.rem(x + 3, 4)
    nxt = lax.rem(sec + 1, 48)
    prv = lax.rem(sec + 47, 48)
    p, cc = (p0, p1), (c0, c1)

    def plane_section(t):
        return lax.div(t, 2) * 6 + zh * 2 + lax.rem(t, 2)

    def beside(k):
        return y * 6 + lax.rem(zh + k, 3) * 2 + c

    def line(k):
        if k == 0:
            return zl
        if k == 1:
            return zl + 1 - 2 * lax.rem(zl, 2)
        if k == 2:
            return zl + 2 - 4 * lax.div(zl, 2)
        return 3 - zl

    def remote(src, dst, ssem, rsem, section, model):
        return pltpu.make_async_remote_copy(
            src_ref=src, dst_ref=dst, send_sem=ssem, recv_sem=rsem,
            device_id=(section, model), device_id_type=MESH)

    own_copy = pltpu.make_async_copy(owner_hbm, owner, own_sem)
    own_copy.start()
    for h in range(2):
        pltpu.make_async_copy(
            e_hbm.at[0, pl.ds(place * PIECE, PIECE), pl.ds(h * HALF, HALF)],
            p[h].at[place], s1_recv.at[h]).start()
    loads = [pltpu.make_async_copy(q_hbm.at[0], q, q_sem)]
    for h in range(2):
        loads.append(pltpu.make_async_copy(wk_hbm.at[:, h], wk.at[h], w_sem.at[0, h]))
        loads.append(pltpu.make_async_copy(wv_hbm.at[:, h], wv.at[h], w_sem.at[1, h]))

    barrier = pltpu.get_barrier_semaphore()

    def greet(section, model):
        pl.semaphore_signal(barrier, inc=1, device_id=(section, model), device_id_type=MESH)

    @pl.loop(1, PLANE)
    def _(i):
        greet(plane_section(lax.rem(place + i, PLANE)), mp)

    greet(beside(1), mp)
    greet(beside(2), mp)
    for k in (1, 2, 3):
        greet(sec, line(k) * 4 + x)
    greet(sec, right)
    greet(sec, left)
    greet(prv, mp)
    for load in loads:
        load.start()
    acck[...] = jnp.zeros_like(acck)
    accv[...] = jnp.zeros_like(accv)
    pl.semaphore_wait(barrier, PLANE - 1 + 2 + 3 + 2 + 1)

    for h in range(2):
        @pl.loop(1, PLANE)
        def _(i):
            t = lax.rem(place + i, PLANE)
            remote(e_hbm.at[0, pl.ds(t * PIECE, PIECE), pl.ds(h * HALF, HALF)],
                   p[h].at[place], s1_send.at[h], s1_recv.at[h], plane_section(t), mp).start()

    own_copy.wait()
    at_place, at_zh = [], []
    for m in range(MICRO):
        o = owner[m]
        at_place.append(lax.div(o, 6) * 2 + lax.rem(o, 2))
        at_zh.append(lax.rem(lax.div(o, 2), 3))
    for h in range(2):
        pltpu.make_async_copy(p[h], p[h], s1_recv.at[h]).wait()
        for m in range(MICRO):
            cc[h][zh, m] = p[h][at_place[m]]
        for k in (1, 2):
            remote(cc[h].at[zh], cc[h].at[zh], s2_send.at[h], s2_recv.at[h], beside(k), mp).start()

    for h in range(2):
        pltpu.make_async_copy(cc[h].at[pl.ds(0, 2)], cc[h].at[pl.ds(0, 2)], s2_recv.at[h]).wait()
        for m in range(MICRO):
            f[h, m] = cc[h][at_zh[m], m]
        rows = pl.ds(place * PIECE, PIECE)

        @pl.loop(1, PLANE)
        def _(i):
            t = lax.rem(place + i, PLANE)
            s = plane_section(t)
            remote(f.at[h, lax.rem(s, MICRO)], e.at[h, mp, rows], s3_send.at[h], s3_recv.at[h], s, mp).start()

        e[h, mp, rows] = f[h, lax.rem(sec, MICRO)]

    def block(h, j):
        return e.at[h, j]

    def ready(h):
        pltpu.make_async_copy(e.at[h, mp, pl.ds(0, ROWS - PIECE)],
                              e.at[h, mp, pl.ds(0, ROWS - PIECE)], s3_recv.at[h]).wait()
        for k in (1, 2, 3):
            remote(block(h, mp), block(h, mp), z_send.at[h], g_recv.at[h, mp], sec, line(k) * 4 + x).start()

    def arrived(h, j):
        pltpu.make_async_copy(block(h, j), block(h, j), g_recv.at[h, j]).wait()

    def to_x(h, j, model):
        remote(block(h, j), block(h, j), x_send.at[h], g_recv.at[h, j], sec, model).start()

    def stage_a(h, k):
        j = line(k) * 4 + x
        if k > 0:
            arrived(h, j)
        to_x(h, j, right)
        to_x(h, j, left)

    def stage_b(h, k):
        j = line(k) * 4
        from_left = j + lax.rem(x + 3, 4)
        from_right = j + lax.rem(x + 1, 4)
        if k % 2 == 0:
            arrived(h, from_left)
            to_x(h, from_left, right)
            arrived(h, from_right)
        else:
            arrived(h, from_right)
            to_x(h, from_right, left)
            arrived(h, from_left)

    def stage_c(h, k):
        j = line(k) * 4
        arrived(h, j + lax.rem(x + 2, 4))
        left_side = jnp.concatenate([e[h, j + i] for i in range(NX)], axis=1)
        for w, acc in ((wk, acck), (wv, accv)):
            rows = w[h, pl.ds(j, NX)].reshape(NX * HALF, HEAD_DIM)
            acc[...] += jnp.dot(left_side, rows, preferred_element_type=F32)

    for h in range(2):
        ready(h)
        if h == 0:
            stage_a(0, 0)
            for load in loads:
                load.wait()
    steps = [(h, k) for h in range(2) for k in range(NZL)]
    for i in range(1, len(steps) + 2):
        if i < len(steps):
            stage_a(*steps[i])
        if i - 1 < len(steps):
            stage_b(*steps[i - 1])
        if i >= 2:
            stage_c(*steps[i - 2])

    keys = acck[...].astype(BF16)
    values = accv[...].astype(BF16)
    size = ROWS // CHUNKS
    for i in range(CHUNKS):
        part = pl.ds(i * size, size)
        scores = lax.dot_general(q[part], keys, (((1,), (1,)), ((), ())),
                                 preferred_element_type=F32) * HEAD_DIM ** (-0.5)
        top = jnp.max(scores, axis=1, keepdims=True)
        raised = jnp.exp(scores - top)
        probs = (raised / jnp.sum(raised, axis=1, keepdims=True)).astype(BF16)
        ctx[part] = jnp.dot(probs, values, preferred_element_type=F32).astype(BF16)
        remote(ctx.at[part], out_hbm.at[0, part], o_send, o_recv, nxt, mp).start()

    for h in range(2):
        whole = p[h].at[pl.ds(0, PLANE - 1)]
        pltpu.make_async_copy(whole, whole, s1_send.at[h]).wait()
        pltpu.make_async_copy(whole, whole, s3_send.at[h]).wait()
        two = cc[h].at[pl.ds(0, 2)]
        pltpu.make_async_copy(two, two, s2_send.at[h]).wait()
        pltpu.make_async_copy(e.at[h, pl.ds(0, 3)], e.at[h, pl.ds(0, 3)], z_send.at[h]).wait()
        pltpu.make_async_copy(e.at[h, pl.ds(0, 12)], e.at[h, pl.ds(0, 12)], x_send.at[h]).wait()
    pltpu.make_async_copy(ctx, ctx, o_send).wait()
    pltpu.make_async_copy(ctx, out_hbm.at[0], o_recv).wait()


def per_device(queries, encoded, key_weight, value_weight, owner):
    wk = key_weight.reshape(NZL * NX, 2, HALF, HEAD_DIM)
    wv = value_weight.reshape(NZL * NX, 2, HALF, HEAD_DIM)
    dma = pltpu.SemaphoreType.DMA
    return pl.pallas_call(
        kernel,
        out_shape=jax.ShapeDtypeStruct((1, ROWS, HEAD_DIM), BF16),
        in_specs=[pl.BlockSpec(memory_space=pl.ANY)] * 5,
        out_specs=pl.BlockSpec(memory_space=pl.ANY),
        scratch_shapes=[
            pltpu.SMEM((MICRO,), jnp.int32),
            pltpu.VMEM((ROWS, HEAD_DIM), BF16),
            pltpu.VMEM((2, NZL * NX, HALF, HEAD_DIM), BF16),
            pltpu.VMEM((2, NZL * NX, HALF, HEAD_DIM), BF16),
            pltpu.VMEM((PLANE, PIECE, HALF), BF16),
            pltpu.VMEM((PLANE, PIECE, HALF), BF16),
            pltpu.VMEM((NZH, MICRO, PIECE, HALF), BF16),
            pltpu.VMEM((NZH, MICRO, PIECE, HALF), BF16),
            pltpu.VMEM((2, MICRO, PIECE, HALF), BF16),
            pltpu.VMEM((2, NZL * NX, ROWS, HALF), BF16),
            pltpu.VMEM((ROWS, HEAD_DIM), F32),
            pltpu.VMEM((ROWS, HEAD_DIM), F32),
            pltpu.VMEM((ROWS, HEAD_DIM), BF16),
            dma, dma, dma((2, 2)),
            dma((2,)), dma((2,)), dma((2,)), dma((2,)), dma((2,)), dma((2,)),
            dma((2,)), dma((2,)), dma((2, NZL * NX)), dma, dma,
        ],
        compiler_params=pltpu.CompilerParams(
            collective_id=0, has_side_effects=True, vmem_limit_bytes=32 * 1024 * 1024),
        cost_estimate=pl.CostEstimate(
            flops=2 * 2 * 256 * 4096 * 256, bytes_accessed=5 * 1024 * 1024, transcendentals=65536),
    )(queries, encoded, wk, wv, owner)


def solution(mesh):
    placed = (
        P("section", None, "mp"),
        P("section", None, "mp"),
        P("section", None, "mp"),
        P("section", None, "mp"),
        P(),
    )
    return jax.shard_map(
        per_device, mesh=mesh, in_specs=placed, out_specs=P("section", None, "mp"), check_vma=False
    )
```

```python
import jax
import jax.numpy as jnp
from jax import lax
from jax.experimental import pallas as pl
from jax.experimental.pallas import tpu as pltpu
from jax.sharding import PartitionSpec as P

MESH = pl.DeviceIdType.MESH
HEAD_DIM = 256
MICRO = 8
NY, NZH, NC = 8, 3, 2
NZL, NX = 4, 4
PLANE = NY * NC
ROWS = 256
PIECE = ROWS // PLANE
HALF = 128
CHUNKS = 4
ORDER = (
    "A0", "A1", "A2", "A3", "B0", "B1", "A4", "A5", "B2", "A6", "B3", "A7", "W",
    "C0", "B4", "C1", "B5", "C2", "B6", "C3", "B7", "C4", "C5", "C6", "C7",
)
F32 = jnp.float32
BF16 = jnp.bfloat16


def kernel(q_hbm, e_hbm, wk_hbm, wv_hbm, owner_hbm, out_hbm,
           owner, q, el, wk, wv, p0, p1, c0, c1, f, e, acck, accv, ctx,
           own_sem, el_sem, q_sem, w_sem, s1_send, s1_recv, s2_send, s2_recv, s3_send, s3_recv,
           z_send, x_send, g_recv, o_send, o_recv):
    sec = lax.axis_index("section")
    mp = lax.axis_index("mp")
    y, zh, c = lax.div(sec, 6), lax.rem(lax.div(sec, 2), 3), lax.rem(sec, 2)
    zl, x = lax.div(mp, 4), lax.rem(mp, 4)
    place = y * 2 + c
    right = zl * 4 + lax.rem(x + 1, 4)
    left = zl * 4 + lax.rem(x + 3, 4)
    nxt = lax.rem(sec + 1, 48)
    prv = lax.rem(sec + 47, 48)
    p, cc = (p0, p1), (c0, c1)

    mates = []
    for dy in (4, 3, 5, 2, 6, 1, 7, 0):
        yy = y + dy
        yy = yy - NY * lax.div(yy, NY)
        pair = lax.rem(zh + NY - yy, 4) * 2
        for cc_ in ((c, 1 - c) if dy else (1 - c,)):
            mates.append((yy * 2 + cc_, yy * 6 + zh * 2 + cc_, pair + cc_))

    def beside(k):
        return y * 6 + lax.rem(zh + k, 3) * 2 + c

    half_of_run = lax.div(zl, 2)
    inner = lax.rem(zl + half_of_run, 2)

    def mirrored(v):
        return v + half_of_run * (3 - 2 * v)

    def line(k):
        return zl if k == 0 else mirrored(1 - inner if k == 1 else k)

    def onward(k):
        return mirrored(2 if k == 1 else 0)

    def remote(src, dst, ssem, rsem, section, model):
        return pltpu.make_async_remote_copy(
            src_ref=src, dst_ref=dst, send_sem=ssem, recv_sem=rsem,
            device_id=(section, model), device_id_type=MESH)

    barrier = pltpu.get_barrier_semaphore()

    def greet(section, model):
        pl.semaphore_signal(barrier, inc=1, device_id=(section, model), device_id_type=MESH)

    greet(beside(1), mp)
    greet(beside(2), mp)
    for _, section, _ in mates:
        greet(section, mp)
    greet(prv, mp)
    greet(sec, lax.rem(zl + 1, 4) * 4 + x)
    greet(sec, lax.rem(zl + 3, 4) * 4 + x)
    greet(sec, right)
    greet(sec, left)

    el_copy = pltpu.make_async_copy(e_hbm.at[0], el, el_sem)
    el_copy.start()
    own_copy = pltpu.make_async_copy(owner_hbm, owner, own_sem)
    own_copy.start()
    loads = [pltpu.make_async_copy(q_hbm.at[0], q, q_sem)]
    for h in range(2):
        loads.append(pltpu.make_async_copy(wk_hbm.at[:, h], wk.at[h], w_sem.at[0, h]))
        loads.append(pltpu.make_async_copy(wv_hbm.at[:, h], wv.at[h], w_sem.at[1, h]))
    for load in loads:
        load.start()
    el_copy.wait()
    mine = pl.ds(pl.multiple_of(place * PIECE, PIECE), PIECE)
    for h in range(2):
        p[h][place] = el[mine, h * HALF:(h + 1) * HALF]
    acck[...] = jnp.zeros_like(acck)
    accv[...] = jnp.zeros_like(accv)
    own_copy.wait()
    at_place, at_zh = [], []
    for m in range(MICRO):
        o = owner[m]
        at_place.append(lax.div(o, 6) * 2 + lax.rem(o, 2))
        at_zh.append(lax.rem(lax.div(o, 2), 3))
    pl.semaphore_wait(barrier, PLANE - 1 + 2 + 2 + 2 + 1)

    for h in range(2):
        for t, section, _ in mates:
            remote(el.at[pl.ds(pl.multiple_of(t * PIECE, PIECE), PIECE), pl.ds(h * HALF, HALF)],
                   p[h].at[place], s1_send.at[h], s1_recv.at[h], section, mp).start()

    for h in range(2):
        whole = p[h].at[pl.ds(0, PLANE - 1)]
        pltpu.make_async_copy(whole, whole, s1_recv.at[h]).wait()
        for m in range(MICRO):
            cc[h][zh, m] = p[h][at_place[m]]
        for k in (1, 2):
            remote(cc[h].at[zh], cc[h].at[zh], s2_send.at[h], s2_recv.at[h], beside(k), mp).start()

    for h in range(2):
        pltpu.make_async_copy(cc[h].at[pl.ds(0, 2)], cc[h].at[pl.ds(0, 2)], s2_recv.at[h]).wait()
        for m in range(MICRO):
            f[h, m] = cc[h][at_zh[m], m]
        for _, section, m in mates:
            remote(f.at[h, m], e.at[h, mp, mine], s3_send.at[h], s3_recv.at[h], section, mp).start()
        e[h, mp, mine] = f[h, lax.rem(sec, MICRO)]

    def block(h, j):
        return e.at[h, j]

    def arrived(h, j):
        pltpu.make_async_copy(block(h, j), block(h, j), g_recv.at[h, j]).wait()

    def to_x(h, j, model):
        remote(block(h, j), block(h, j), x_send.at[h], g_recv.at[h, j], sec, model).start()

    def to_z(h, j, run):
        remote(block(h, j), block(h, j), z_send.at[h], g_recv.at[h, j], sec, run * 4 + x).start()

    def stage_a(h, k):
        j = line(k) * 4 + x
        if k == 0:
            others = e.at[h, mp, pl.ds(0, ROWS - PIECE)]
            pltpu.make_async_copy(others, others, s3_recv.at[h]).wait()

            @pl.when(zl < NZL - 1)
            def _():
                to_z(h, j, zl + 1)

            @pl.when(zl > 0)
            def _():
                to_z(h, j, zl - 1)
        else:
            arrived(h, j)

            @pl.when(inner == 1)
            def _():
                to_z(h, j, onward(k))

        to_x(h, j, right)
        to_x(h, j, left)

    def stage_b(h, k):
        j = line(k) * 4
        from_left = j + lax.rem(x + 3, 4)
        from_right = j + lax.rem(x + 1, 4)
        if k % 2 == 0:
            arrived(h, from_left)
            to_x(h, from_left, right)
            arrived(h, from_right)
        else:
            arrived(h, from_right)
            to_x(h, from_right, left)
            arrived(h, from_left)

    def stage_c(h, k):
        j = line(k) * 4
        arrived(h, j + lax.rem(x + 2, 4))
        left_side = jnp.concatenate([e[h, j + i] for i in range(NX)], axis=1)
        for w, acc in ((wk, acck), (wv, accv)):
            rows = w[h, pl.ds(j, NX)].reshape(NX * HALF, HEAD_DIM)
            acc[...] += jnp.dot(left_side, rows, preferred_element_type=F32)

    steps = [(h, k) for k in range(NZL) for h in range(2)]
    for step in ORDER:
        if step == "W":
            for load in loads:
                load.wait()
        else:
            {"A": stage_a, "B": stage_b, "C": stage_c}[step[0]](*steps[int(step[1])])

    keys = acck[...].astype(BF16)
    values = accv[...].astype(BF16)
    size = ROWS // CHUNKS
    for i in range(CHUNKS):
        part = pl.ds(i * size, size)
        scores = lax.dot_general(q[part], keys, (((1,), (1,)), ((), ())),
                                 preferred_element_type=F32) * HEAD_DIM ** (-0.5)
        top = jnp.max(scores, axis=1, keepdims=True)
        raised = jnp.exp(scores - top)
        probs = (raised / jnp.sum(raised, axis=1, keepdims=True)).astype(BF16)
        ctx[part] = jnp.dot(probs, values, preferred_element_type=F32).astype(BF16)
        remote(ctx.at[part], out_hbm.at[0, part], o_send, o_recv, nxt, mp).start()

    for h in range(2):
        whole = p[h].at[pl.ds(0, PLANE - 1)]
        pltpu.make_async_copy(whole, whole, s1_send.at[h]).wait()
        pltpu.make_async_copy(whole, whole, s3_send.at[h]).wait()
        two = cc[h].at[pl.ds(0, 2)]
        pltpu.make_async_copy(two, two, s2_send.at[h]).wait()
        one = e.at[h, 0]
        pltpu.make_async_copy(one, one, z_send.at[h]).wait()

        @pl.when(inner == 1)
        def _():
            four = e.at[h, pl.ds(0, 4)]
            pltpu.make_async_copy(four, four, z_send.at[h]).wait()

        pltpu.make_async_copy(e.at[h, pl.ds(0, 12)], e.at[h, pl.ds(0, 12)], x_send.at[h]).wait()
    pltpu.make_async_copy(ctx, ctx, o_send).wait()
    pltpu.make_async_copy(ctx, out_hbm.at[0], o_recv).wait()


def per_device(queries, encoded, key_weight, value_weight, owner):
    wk = key_weight.reshape(NZL * NX, 2, HALF, HEAD_DIM)
    wv = value_weight.reshape(NZL * NX, 2, HALF, HEAD_DIM)
    dma = pltpu.SemaphoreType.DMA
    return pl.pallas_call(
        kernel,
        out_shape=jax.ShapeDtypeStruct((1, ROWS, HEAD_DIM), BF16),
        in_specs=[pl.BlockSpec(memory_space=pl.ANY)] * 5,
        out_specs=pl.BlockSpec(memory_space=pl.ANY),
        scratch_shapes=[
            pltpu.SMEM((MICRO,), jnp.int32),
            pltpu.VMEM((ROWS, HEAD_DIM), BF16),
            pltpu.VMEM((ROWS, HEAD_DIM), BF16),
            pltpu.VMEM((2, NZL * NX, HALF, HEAD_DIM), BF16),
            pltpu.VMEM((2, NZL * NX, HALF, HEAD_DIM), BF16),
            pltpu.VMEM((PLANE, PIECE, HALF), BF16),
            pltpu.VMEM((PLANE, PIECE, HALF), BF16),
            pltpu.VMEM((NZH, MICRO, PIECE, HALF), BF16),
            pltpu.VMEM((NZH, MICRO, PIECE, HALF), BF16),
            pltpu.VMEM((2, MICRO, PIECE, HALF), BF16),
            pltpu.VMEM((2, NZL * NX, ROWS, HALF), BF16),
            pltpu.VMEM((ROWS, HEAD_DIM), F32),
            pltpu.VMEM((ROWS, HEAD_DIM), F32),
            pltpu.VMEM((ROWS, HEAD_DIM), BF16),
            dma, dma, dma, dma((2, 2)),
            dma((2,)), dma((2,)), dma((2,)), dma((2,)), dma((2,)), dma((2,)),
            dma((2,)), dma((2,)), dma((2, NZL * NX)), dma, dma,
        ],
        compiler_params=pltpu.CompilerParams(
            collective_id=0, has_side_effects=True, vmem_limit_bytes=60 * 1024 * 1024),
        cost_estimate=pl.CostEstimate(
            flops=2 * 2 * 256 * 4096 * 256, bytes_accessed=5 * 1024 * 1024, transcendentals=65536),
    )(queries, encoded, wk, wv, owner)


def solution(mesh):
    placed = (
        P("section", None, "mp"),
        P("section", None, "mp"),
        P("section", None, "mp"),
        P("section", None, "mp"),
        P(),
    )
    return jax.shard_map(
        per_device, mesh=mesh, in_specs=placed, out_specs=P("section", None, "mp"), check_vma=False
    )
```

```python
import jax
import jax.numpy as jnp
from jax import lax
from jax.experimental import pallas as pl
from jax.experimental.pallas import tpu as pltpu
from jax.sharding import PartitionSpec as P

MESH = pl.DeviceIdType.MESH
HEAD_DIM = 256
MICRO = 8
NY, NZH, NC = 8, 3, 2
NZL, NX = 4, 4
PLANE = NY * NC
ROWS = 256
PIECE = ROWS // PLANE
HALF = 128
CHUNKS = 2
ORDER = (
    "P0", "P1", "N", "Q0", "Q1", "R0", "R1", "A0", "A1", "A2", "A3", "B0", "B1",
    "A4", "A5", "B2", "A6", "B3", "A7", "W", "C0", "B4", "C1", "B5", "C2", "B6",
    "C3", "B7", "C4", "C5", "C6", "C7",
)
F32 = jnp.float32
BF16 = jnp.bfloat16


def kernel(q_hbm, e_hbm, wk_hbm, wv_hbm, owner_hbm, out_hbm,
           owner, q, el, wk, wv, p0, p1, c0, c1, f, e, acck, accv, ctx,
           own_sem, el_sem, q_sem, w_sem, s1_send, s1_recv, s2_send, s2_recv, s3_send, s3_recv,
           z_send, x_send, g_recv, o_send, o_recv):
    sec = lax.axis_index("section")
    mp = lax.axis_index("mp")
    y, zh, c = lax.div(sec, 6), lax.rem(lax.div(sec, 2), 3), lax.rem(sec, 2)
    zl, x = lax.div(mp, 4), lax.rem(mp, 4)
    place = y * 2 + c
    right = zl * 4 + lax.rem(x + 1, 4)
    left = zl * 4 + lax.rem(x + 3, 4)
    nxt = lax.rem(sec + 1, 48)
    prv = lax.rem(sec + 47, 48)
    p, cc = (p0, p1), (c0, c1)

    mates = []
    for dy in (4, 3, 5, 2, 6, 1, 7, 0):
        yy = y + dy
        yy = yy - NY * lax.div(yy, NY)
        pair = lax.rem(zh + NY - yy, 4) * 2
        for cc_ in ((c, 1 - c) if dy else (1 - c,)):
            mates.append((yy * 2 + cc_, yy * 6 + zh * 2 + cc_, pair + cc_))

    def beside(k):
        return y * 6 + lax.rem(zh + k, 3) * 2 + c

    half_of_run = lax.div(zl, 2)
    inner = lax.rem(zl + half_of_run, 2)

    def mirrored(v):
        return v + half_of_run * (3 - 2 * v)

    def line(k):
        return zl if k == 0 else mirrored(1 - inner if k == 1 else k)

    def onward(k):
        return mirrored(2 if k == 1 else 0)

    def remote(src, dst, ssem, rsem, section, model):
        return pltpu.make_async_remote_copy(
            src_ref=src, dst_ref=dst, send_sem=ssem, recv_sem=rsem,
            device_id=(section, model), device_id_type=MESH)

    barrier = pltpu.get_barrier_semaphore()

    def greet(section, model):
        pl.semaphore_signal(barrier, inc=1, device_id=(section, model), device_id_type=MESH)

    el_copy = pltpu.make_async_copy(e_hbm.at[0], el, el_sem)
    el_copy.start()
    own_copy = pltpu.make_async_copy(owner_hbm, owner, own_sem)
    own_copy.start()
    for _, section, _ in mates:
        greet(section, mp)
    greet(beside(1), mp)
    greet(beside(2), mp)
    greet(prv, mp)
    greet(sec, lax.rem(zl + 1, 4) * 4 + x)
    greet(sec, lax.rem(zl + 3, 4) * 4 + x)
    greet(sec, right)
    greet(sec, left)
    loads = [pltpu.make_async_copy(q_hbm.at[0], q, q_sem)]
    for h in range(2):
        loads.append(pltpu.make_async_copy(wk_hbm.at[:, h], wk.at[h], w_sem.at[0, h]))
        loads.append(pltpu.make_async_copy(wv_hbm.at[:, h], wv.at[h], w_sem.at[1, h]))
    mine = pl.ds(pl.multiple_of(place * PIECE, PIECE), PIECE)
    at_place, at_zh = [], []

    def stage_n():
        for load in loads:
            load.start()
        for h in range(2):
            p[h][place] = el[mine, h * HALF:(h + 1) * HALF]
        acck[...] = jnp.zeros_like(acck)
        accv[...] = jnp.zeros_like(accv)
        own_copy.wait()
        for m in range(MICRO):
            o = owner[m]
            at_place.append(lax.div(o, 6) * 2 + lax.rem(o, 2))
            at_zh.append(lax.rem(lax.div(o, 2), 3))

    el_copy.wait()
    pl.semaphore_wait(barrier, PLANE - 1 + 2 + 2 + 2 + 1)

    def stage_p(h):
        for t, section, _ in mates:
            remote(el.at[pl.ds(pl.multiple_of(t * PIECE, PIECE), PIECE), pl.ds(h * HALF, HALF)],
                   p[h].at[place], s1_send.at[h], s1_recv.at[h], section, mp).start()

    def stage_q(h):
        whole = p[h].at[pl.ds(0, PLANE - 1)]
        pltpu.make_async_copy(whole, whole, s1_recv.at[h]).wait()
        for m in range(MICRO):
            cc[h][zh, m] = p[h][at_place[m]]
        for k in (1, 2):
            remote(cc[h].at[zh], cc[h].at[zh], s2_send.at[h], s2_recv.at[h], beside(k), mp).start()

    def stage_r(h):
        two = cc[h].at[pl.ds(0, 2)]
        pltpu.make_async_copy(two, two, s2_recv.at[h]).wait()
        for m in range(MICRO):
            f[h, m] = cc[h][at_zh[m], m]
        for _, section, m in mates:
            remote(f.at[h, m], e.at[h, mp, mine], s3_send.at[h], s3_recv.at[h], section, mp).start()
        e[h, mp, mine] = f[h, lax.rem(sec, MICRO)]

    def block(h, j):
        return e.at[h, j]

    def arrived(h, j):
        pltpu.make_async_copy(block(h, j), block(h, j), g_recv.at[h, j]).wait()

    def to_x(h, j, model):
        remote(block(h, j), block(h, j), x_send.at[h], g_recv.at[h, j], sec, model).start()

    def to_z(h, j, run):
        remote(block(h, j), block(h, j), z_send.at[h], g_recv.at[h, j], sec, run * 4 + x).start()

    def stage_a(h, k):
        j = line(k) * 4 + x
        if k == 0:
            others = e.at[h, mp, pl.ds(0, ROWS - PIECE)]
            pltpu.make_async_copy(others, others, s3_recv.at[h]).wait()

            @pl.when(zl < NZL - 1)
            def _():
                to_z(h, j, zl + 1)

            @pl.when(zl > 0)
            def _():
                to_z(h, j, zl - 1)
        else:
            arrived(h, j)

            @pl.when(inner == 1)
            def _():
                to_z(h, j, onward(k))

        to_x(h, j, right)
        to_x(h, j, left)

    def stage_b(h, k):
        j = line(k) * 4
        if (h + k) % 2 == 0:
            j += lax.rem(x + 3, 4)
            arrived(h, j)
            to_x(h, j, right)
        else:
            j += lax.rem(x + 1, 4)
            arrived(h, j)
            to_x(h, j, left)

    def stage_c(h, k):
        j = line(k) * 4
        arrived(h, j + lax.rem(x + (1 if (h + k) % 2 == 0 else 3), 4))
        arrived(h, j + lax.rem(x + 2, 4))
        left_side = jnp.concatenate([e[h, j + i] for i in range(NX)], axis=1)
        for w, acc in ((wk, acck), (wv, accv)):
            rows = w[h, pl.ds(j, NX)].reshape(NX * HALF, HEAD_DIM)
            acc[...] += jnp.dot(left_side, rows, preferred_element_type=F32)

    steps = [(h, k) for k in range(NZL) for h in range(2)]
    for step in ORDER:
        if step == "W":
            for load in loads:
                load.wait()
        elif step == "N":
            stage_n()
        elif step[0] in "PQR":
            {"P": stage_p, "Q": stage_q, "R": stage_r}[step[0]](int(step[1]))
        else:
            {"A": stage_a, "B": stage_b, "C": stage_c}[step[0]](*steps[int(step[1])])

    keys = acck[...].astype(BF16)
    values = accv[...].astype(BF16)
    size = ROWS // CHUNKS
    for i in range(CHUNKS):
        part = pl.ds(i * size, size)
        scores = lax.dot_general(q[part], keys, (((1,), (1,)), ((), ())),
                                 preferred_element_type=F32) * HEAD_DIM ** (-0.5)
        top = jnp.max(scores, axis=1, keepdims=True)
        raised = jnp.exp(scores - top)
        probs = (raised / jnp.sum(raised, axis=1, keepdims=True)).astype(BF16)
        ctx[part] = jnp.dot(probs, values, preferred_element_type=F32).astype(BF16)
        remote(ctx.at[part], out_hbm.at[0, part], o_send, o_recv, nxt, mp).start()

    for h in range(2):
        whole = p[h].at[pl.ds(0, PLANE - 1)]
        pltpu.make_async_copy(whole, whole, s1_send.at[h]).wait()
        pltpu.make_async_copy(whole, whole, s3_send.at[h]).wait()
        two = cc[h].at[pl.ds(0, 2)]
        pltpu.make_async_copy(two, two, s2_send.at[h]).wait()
        one = e.at[h, 0]
        pltpu.make_async_copy(one, one, z_send.at[h]).wait()

        @pl.when(inner == 1)
        def _():
            four = e.at[h, pl.ds(0, 4)]
            pltpu.make_async_copy(four, four, z_send.at[h]).wait()

        pltpu.make_async_copy(e.at[h, pl.ds(0, 12)], e.at[h, pl.ds(0, 12)], x_send.at[h]).wait()
    pltpu.make_async_copy(ctx, ctx, o_send).wait()
    pltpu.make_async_copy(ctx, out_hbm.at[0], o_recv).wait()


def per_device(queries, encoded, key_weight, value_weight, owner):
    wk = key_weight.reshape(NZL * NX, 2, HALF, HEAD_DIM)
    wv = value_weight.reshape(NZL * NX, 2, HALF, HEAD_DIM)
    dma = pltpu.SemaphoreType.DMA
    return pl.pallas_call(
        kernel,
        out_shape=jax.ShapeDtypeStruct((1, ROWS, HEAD_DIM), BF16),
        in_specs=[pl.BlockSpec(memory_space=pl.ANY)] * 5,
        out_specs=pl.BlockSpec(memory_space=pl.ANY),
        scratch_shapes=[
            pltpu.SMEM((MICRO,), jnp.int32),
            pltpu.VMEM((ROWS, HEAD_DIM), BF16),
            pltpu.VMEM((ROWS, HEAD_DIM), BF16),
            pltpu.VMEM((2, NZL * NX, HALF, HEAD_DIM), BF16),
            pltpu.VMEM((2, NZL * NX, HALF, HEAD_DIM), BF16),
            pltpu.VMEM((PLANE, PIECE, HALF), BF16),
            pltpu.VMEM((PLANE, PIECE, HALF), BF16),
            pltpu.VMEM((NZH, MICRO, PIECE, HALF), BF16),
            pltpu.VMEM((NZH, MICRO, PIECE, HALF), BF16),
            pltpu.VMEM((2, MICRO, PIECE, HALF), BF16),
            pltpu.VMEM((2, NZL * NX, ROWS, HALF), BF16),
            pltpu.VMEM((ROWS, HEAD_DIM), F32),
            pltpu.VMEM((ROWS, HEAD_DIM), F32),
            pltpu.VMEM((ROWS, HEAD_DIM), BF16),
            dma, dma, dma, dma((2, 2)),
            dma((2,)), dma((2,)), dma((2,)), dma((2,)), dma((2,)), dma((2,)),
            dma((2,)), dma((2,)), dma((2, NZL * NX)), dma, dma,
        ],
        compiler_params=pltpu.CompilerParams(
            collective_id=0, has_side_effects=True, vmem_limit_bytes=60 * 1024 * 1024),
        cost_estimate=pl.CostEstimate(
            flops=2 * 2 * 256 * 4096 * 256, bytes_accessed=5 * 1024 * 1024, transcendentals=65536),
    )(queries, encoded, wk, wv, owner)


def solution(mesh):
    placed = (
        P("section", None, "mp"),
        P("section", None, "mp"),
        P("section", None, "mp"),
        P("section", None, "mp"),
        P(),
    )
    return jax.shard_map(
        per_device, mesh=mesh, in_specs=placed, out_specs=P("section", None, "mp"), check_vma=False
    )
```

```python
import jax
import jax.numpy as jnp
from jax import lax
from jax.experimental import pallas as pl
from jax.experimental.pallas import tpu as pltpu
from jax.sharding import PartitionSpec as P

MESH = pl.DeviceIdType.MESH
HEAD_DIM = 256
MICRO = 8
NY, NZH, NC = 8, 3, 2
NZL, NX = 4, 4
PLANE = NY * NC
ROWS = 256
PIECE = ROWS // PLANE
HALF = 128
CHUNKS = 2
ORDER = (
    "P0", "P1", "N", "Q0", "Q1", "R0", "R1", "A0", "A1", "A2", "B0", "A3", "B1",
    "A4", "A5", "B2", "A6", "B3", "A7", "B4", "W", "C0", "B5", "C1", "B6", "C2",
    "B7", "C3", "C4", "C5", "C6", "C7",
)
F32 = jnp.float32
BF16 = jnp.bfloat16


def kernel(q_hbm, e_hbm, wk_hbm, wv_hbm, owner_hbm, out_hbm,
           owner, q, el, wk, wv, p0, p1, c0, c1, f, e, acck, accv, ctx,
           own_sem, el_sem, q_sem, w_sem, s1_send, s1_recv, s2_send, s2_recv, s3_send, s3_recv,
           z_send, x_send, g_recv, o_send, o_recv):
    sec = lax.axis_index("section")
    mp = lax.axis_index("mp")
    y, zh, c = lax.div(sec, 6), lax.rem(lax.div(sec, 2), 3), lax.rem(sec, 2)
    zl, x = lax.div(mp, 4), lax.rem(mp, 4)
    place = y * 2 + c
    right = zl * 4 + lax.rem(x + 1, 4)
    left = zl * 4 + lax.rem(x + 3, 4)
    nxt = lax.rem(sec + 1, 48)
    prv = lax.rem(sec + 47, 48)
    p, cc = (p0, p1), (c0, c1)

    mates = []
    for dy in (4, 3, 5, 2, 6, 1, 7, 0):
        yy = y + dy
        yy = yy - NY * lax.div(yy, NY)
        pair = lax.rem(zh + NY - yy, 4) * 2
        for cc_ in ((c, 1 - c) if dy else (1 - c,)):
            mates.append((yy * 2 + cc_, yy * 6 + zh * 2 + cc_, pair + cc_))

    def beside(k):
        return y * 6 + lax.rem(zh + k, 3) * 2 + c

    half_of_run = lax.div(zl, 2)
    inner = lax.rem(zl + half_of_run, 2)

    def mirrored(v):
        return v + half_of_run * (3 - 2 * v)

    def line(k):
        return zl if k == 0 else mirrored(1 - inner if k == 1 else k)

    def onward(k):
        return mirrored(2 if k == 1 else 0)

    def remote(src, dst, ssem, rsem, section, model):
        return pltpu.make_async_remote_copy(
            src_ref=src, dst_ref=dst, send_sem=ssem, recv_sem=rsem,
            device_id=(section, model), device_id_type=MESH)

    barrier = pltpu.get_barrier_semaphore()

    def greet(section, model):
        pl.semaphore_signal(barrier, inc=1, device_id=(section, model), device_id_type=MESH)

    el_copy = pltpu.make_async_copy(e_hbm.at[0], el, el_sem)
    el_copy.start()
    own_copy = pltpu.make_async_copy(owner_hbm, owner, own_sem)
    own_copy.start()
    for _, section, _ in mates:
        greet(section, mp)
    greet(beside(1), mp)
    greet(beside(2), mp)
    greet(prv, mp)
    greet(sec, lax.rem(zl + 1, 4) * 4 + x)
    greet(sec, lax.rem(zl + 3, 4) * 4 + x)
    greet(sec, right)
    greet(sec, left)
    loads = [pltpu.make_async_copy(q_hbm.at[0], q, q_sem)]
    for h in range(2):
        loads.append(pltpu.make_async_copy(wk_hbm.at[:, h], wk.at[h], w_sem.at[0, h]))
        loads.append(pltpu.make_async_copy(wv_hbm.at[:, h], wv.at[h], w_sem.at[1, h]))
    mine = pl.ds(pl.multiple_of(place * PIECE, PIECE), PIECE)
    at_place, at_zh = [], []

    def stage_n():
        for load in loads:
            load.start()
        for h in range(2):
            p[h][place] = el[mine, h * HALF:(h + 1) * HALF]
        acck[...] = jnp.zeros_like(acck)
        accv[...] = jnp.zeros_like(accv)
        own_copy.wait()
        for m in range(MICRO):
            o = owner[m]
            at_place.append(lax.div(o, 6) * 2 + lax.rem(o, 2))
            at_zh.append(lax.rem(lax.div(o, 2), 3))

    el_copy.wait()
    pl.semaphore_wait(barrier, PLANE - 1 + 2 + 2 + 2 + 1)

    def stage_p(h):
        for t, section, _ in mates:
            remote(el.at[pl.ds(pl.multiple_of(t * PIECE, PIECE), PIECE), pl.ds(h * HALF, HALF)],
                   p[h].at[place], s1_send.at[h], s1_recv.at[h], section, mp).start()

    def stage_q(h):
        whole = p[h].at[pl.ds(0, PLANE - 1)]
        pltpu.make_async_copy(whole, whole, s1_recv.at[h]).wait()
        for m in range(MICRO):
            cc[h][zh, m] = p[h][at_place[m]]
        for k in (1, 2):
            remote(cc[h].at[zh], cc[h].at[zh], s2_send.at[h], s2_recv.at[h], beside(k), mp).start()

    def stage_r(h):
        two = cc[h].at[pl.ds(0, 2)]
        pltpu.make_async_copy(two, two, s2_recv.at[h]).wait()
        for m in range(MICRO):
            f[h, m] = cc[h][at_zh[m], m]
        for _, section, m in mates:
            remote(f.at[h, m], e.at[h, mp, mine], s3_send.at[h], s3_recv.at[h], section, mp).start()
        e[h, mp, mine] = f[h, lax.rem(sec, MICRO)]

    def block(h, j):
        return e.at[h, j]

    def arrived(h, j):
        pltpu.make_async_copy(block(h, j), block(h, j), g_recv.at[h, j]).wait()

    def to_x(h, j, model):
        remote(block(h, j), block(h, j), x_send.at[h], g_recv.at[h, j], sec, model).start()

    def to_z(h, j, run):
        remote(block(h, j), block(h, j), z_send.at[h], g_recv.at[h, j], sec, run * 4 + x).start()

    def stage_a(h, k):
        j = line(k) * 4 + x
        if k == 0:
            others = e.at[h, mp, pl.ds(0, ROWS - PIECE)]
            pltpu.make_async_copy(others, others, s3_recv.at[h]).wait()

            @pl.when(zl < NZL - 1)
            def _():
                to_z(h, j, zl + 1)

            @pl.when(zl > 0)
            def _():
                to_z(h, j, zl - 1)
        else:
            arrived(h, j)

            @pl.when(inner == 1)
            def _():
                to_z(h, j, onward(k))

        to_x(h, j, right)
        to_x(h, j, left)

    def stage_b(h, k):
        j = line(k) * 4
        if (h + k) % 2 == 0:
            j += lax.rem(x + 3, 4)
            arrived(h, j)
            to_x(h, j, right)
        else:
            j += lax.rem(x + 1, 4)
            arrived(h, j)
            to_x(h, j, left)

    def stage_c(h, k):
        j = line(k) * 4
        arrived(h, j + lax.rem(x + (1 if (h + k) % 2 == 0 else 3), 4))
        arrived(h, j + lax.rem(x + 2, 4))
        left_side = jnp.concatenate([e[h, j + i] for i in range(NX)], axis=1)
        for w, acc in ((wk, acck), (wv, accv)):
            rows = w[h, pl.ds(j, NX)].reshape(NX * HALF, HEAD_DIM)
            acc[...] += jnp.dot(left_side, rows, preferred_element_type=F32)

    steps = [(h, k) for k in range(NZL) for h in range(2)]
    for step in ORDER:
        if step == "W":
            for load in loads:
                load.wait()
        elif step == "N":
            stage_n()
        elif step[0] in "PQR":
            {"P": stage_p, "Q": stage_q, "R": stage_r}[step[0]](int(step[1]))
        else:
            {"A": stage_a, "B": stage_b, "C": stage_c}[step[0]](*steps[int(step[1])])

    keys = acck[...].astype(BF16)
    values = accv[...].astype(BF16)
    size = ROWS // CHUNKS
    for i in range(CHUNKS):
        part = pl.ds(i * size, size)
        scores = lax.dot_general(q[part], keys, (((1,), (1,)), ((), ())),
                                 preferred_element_type=F32) * HEAD_DIM ** (-0.5)
        top = jnp.max(scores, axis=1, keepdims=True)
        raised = jnp.exp(scores - top)
        probs = (raised / jnp.sum(raised, axis=1, keepdims=True)).astype(BF16)
        ctx[part] = jnp.dot(probs, values, preferred_element_type=F32).astype(BF16)
        remote(ctx.at[part], out_hbm.at[0, part], o_send, o_recv, nxt, mp).start()

    for h in range(2):
        whole = p[h].at[pl.ds(0, PLANE - 1)]
        pltpu.make_async_copy(whole, whole, s1_send.at[h]).wait()
        pltpu.make_async_copy(whole, whole, s3_send.at[h]).wait()
        two = cc[h].at[pl.ds(0, 2)]
        pltpu.make_async_copy(two, two, s2_send.at[h]).wait()
        one = e.at[h, 0]
        pltpu.make_async_copy(one, one, z_send.at[h]).wait()

        @pl.when(inner == 1)
        def _():
            four = e.at[h, pl.ds(0, 4)]
            pltpu.make_async_copy(four, four, z_send.at[h]).wait()

        pltpu.make_async_copy(e.at[h, pl.ds(0, 12)], e.at[h, pl.ds(0, 12)], x_send.at[h]).wait()
    pltpu.make_async_copy(ctx, ctx, o_send).wait()
    pltpu.make_async_copy(ctx, out_hbm.at[0], o_recv).wait()


def per_device(queries, encoded, key_weight, value_weight, owner):
    wk = key_weight.reshape(NZL * NX, 2, HALF, HEAD_DIM)
    wv = value_weight.reshape(NZL * NX, 2, HALF, HEAD_DIM)
    dma = pltpu.SemaphoreType.DMA
    return pl.pallas_call(
        kernel,
        out_shape=jax.ShapeDtypeStruct((1, ROWS, HEAD_DIM), BF16),
        in_specs=[pl.BlockSpec(memory_space=pl.ANY)] * 5,
        out_specs=pl.BlockSpec(memory_space=pl.ANY),
        scratch_shapes=[
            pltpu.SMEM((MICRO,), jnp.int32),
            pltpu.VMEM((ROWS, HEAD_DIM), BF16),
            pltpu.VMEM((ROWS, HEAD_DIM), BF16),
            pltpu.VMEM((2, NZL * NX, HALF, HEAD_DIM), BF16),
            pltpu.VMEM((2, NZL * NX, HALF, HEAD_DIM), BF16),
            pltpu.VMEM((PLANE, PIECE, HALF), BF16),
            pltpu.VMEM((PLANE, PIECE, HALF), BF16),
            pltpu.VMEM((NZH, MICRO, PIECE, HALF), BF16),
            pltpu.VMEM((NZH, MICRO, PIECE, HALF), BF16),
            pltpu.VMEM((2, MICRO, PIECE, HALF), BF16),
            pltpu.VMEM((2, NZL * NX, ROWS, HALF), BF16),
            pltpu.VMEM((ROWS, HEAD_DIM), F32),
            pltpu.VMEM((ROWS, HEAD_DIM), F32),
            pltpu.VMEM((ROWS, HEAD_DIM), BF16),
            dma, dma, dma, dma((2, 2)),
            dma((2,)), dma((2,)), dma((2,)), dma((2,)), dma((2,)), dma((2,)),
            dma((2,)), dma((2,)), dma((2, NZL * NX)), dma, dma,
        ],
        compiler_params=pltpu.CompilerParams(
            collective_id=0, has_side_effects=True, vmem_limit_bytes=60 * 1024 * 1024),
        cost_estimate=pl.CostEstimate(
            flops=2 * 2 * 256 * 4096 * 256, bytes_accessed=5 * 1024 * 1024, transcendentals=65536),
    )(queries, encoded, wk, wv, owner)


def solution(mesh):
    placed = (
        P("section", None, "mp"),
        P("section", None, "mp"),
        P("section", None, "mp"),
        P("section", None, "mp"),
        P(),
    )
    return jax.shard_map(
        per_device, mesh=mesh, in_specs=placed, out_specs=P("section", None, "mp"), check_vma=False
    )
```
